512 devices in a mesh: rep: 32 (over x, z_lo, core), fsdp: 16 (over y, z_hi).
Axes of the slice: x: 4, y: 8, z: 8 (z_hi: 2, z_lo: 4; z = z_hi * 4 + z_lo), core: 2. Of those that a mesh axis runs over, the one named last changes fastest.
Arguments:
- inputs: bfloat16 [32, 4096, 2304], P('rep', 'fsdp'), may hold values from -6 to 6
- cotangent: bfloat16 [32, 4096, 1024], P('rep', 'fsdp'), may hold values from -6 to 6
- params: float32 [32, 2304, 1024], P('rep', 'fsdp'), may hold values from -6 to 6
- moment: float32 [32, 2304, 1024], P('rep', 'fsdp'), may hold values from -1.2 to 1.2
- second: float32 [32, 2304, 1024], P('rep', 'fsdp'), may hold values from 0.02 to 0.5
- drift: bfloat16 [32, 2304, 1024], P('rep', 'fsdp'), may hold values from -12 to 12
- anchor: float32 [2304, 1024], P('fsdp', 'rep'), may hold values from -6 to 6
- momentum: float32 [2304, 1024], P('fsdp', 'rep'), may hold values from -6 to 6
Outputs:
- merged: float32 [32, 2304, 1024], P('rep', 'fsdp')
- keys: bfloat16 [32, 4096, 1024], P('rep', 'fsdp')
- anchor_new: float32 [2304, 1024], P('fsdp', 'rep')
- momentum_new: float32 [2304, 1024], P('fsdp', 'rep')
The draws below stay inside these ranges and needn't reach their ends.
All inputs are finite; a program needn't handle non-finite values.
Results may differ from the reference program's by a relative error of at most 0.005.
Values may be sent and summed in bfloat16 or wider, within the bound.
No kernel may reach another device: no remote copies, remote signals or barrier semaphores. Data moves between devices by JAX's collectives and lax.ppermute only.
A program may use at most 64 MiB of HBM per device.

```python
import math
import jax
import jax.numpy as jnp
from jax import lax

D = 2304
HEAD_DIM = 128
KV = 1024
TOK = 4096
REPS = 32


def strengthened(result, rng, source, target, blocks, factor):
    def block_of(position):
        return (jnp.arange(result.shape[position]) // (result.shape[position] // blocks)).reshape((-1,) + (1,) * (result.ndim - 1 - position))

    first = jax.random.permutation(rng, blocks)[block_of(target)]
    second = (block_of(target) + blocks // 2) % blocks
    return jnp.where((block_of(source) == first) | (block_of(source) == second), factor * result, result)


def levels(stream_key, shape, split, least, top_value):
    loudness = 1.0
    for axis_at, shards_of in split:
        draws = jax.random.uniform(jax.random.fold_in(jax.random.fold_in(stream_key, 6), axis_at), (shards_of,), jnp.float32, least / len(split), top_value / len(split))
        loudness = loudness * jnp.repeat(jnp.exp(draws), shape[axis_at] // shards_of).reshape((-1,) + (1,) * (len(shape) - 1 - axis_at))
    return loudness


def noise(own_key, extent, spread, bound, split=(), held_as=jnp.bfloat16):
    values = jax.random.normal(own_key, extent, jnp.float32) * spread
    if len(split) > 0:
        values = levels(own_key, extent, split, -0.22, 0.18) * values
    return jnp.clip(values, min=-bound, max=bound).astype(held_as)


def heavy_noise(stream_key, shape, deviation, limit, pieces, heavy, kind=jnp.bfloat16):
    drawn = deviation * jax.random.normal(stream_key, shape, jnp.float32)
    if pieces:
        drawn = drawn * levels(stream_key, shape, pieces, -0.22, 0.18)
    return jnp.clip(strengthened(drawn, jax.random.fold_in(stream_key, 3), *heavy), -limit, limit).astype(kind)


def setup_inputs(seed: int = 0) -> dict:
    splits = jax.random.split(jax.random.key(seed), 9)
    inputs = noise(splits[0], (REPS, TOK, D), 1.0, 6.0, ((0, 32), (1, 16)))
    cotangent = noise(splits[1], (REPS, TOK, KV), 1.0, 6.0, ((0, 32), (1, 16)))
    params = noise(splits[2], (REPS, D, KV), 1.0, 6.0, ((0, 32), (1, 16)), jnp.float32)
    moment = noise(splits[3], (REPS, D, KV), 0.2, 1.2, ((0, 32), (1, 16)), jnp.float32)
    second = jnp.clip(jnp.exp(math.log(0.5) - 3.218876 * jax.random.uniform(splits[4], (REPS, D, KV), jnp.float32) ** levels(splits[4], (REPS, D, KV), ((0, 32), (1, 16)), -0.2, 0.2)), 0.02, 0.5)
    drift = heavy_noise(splits[5], (REPS, D, KV), 2.0, 12.0, ((0, 32), (1, 16)), (0, 2, 32, 2.75))
    anchor = noise(splits[6], (D, KV), 1.0, 6.0, ((0, 16), (1, 32)), jnp.float32)
    momentum = noise(splits[7], (D, KV), 1.0, 6.0, ((0, 16), (1, 32)), jnp.float32)
    return {"inputs": inputs, "cotangent": cotangent, "params": params, "moment": moment, "second": second, "drift": drift, "anchor": anchor, "momentum": momentum}


def norm_backward(projected, upstream):
    rows = projected.shape[0]
    heads_view = projected.reshape(rows, -1, HEAD_DIM)
    grads_view = upstream.reshape(rows, -1, HEAD_DIM)
    rms = jnp.sqrt(lax.optimization_barrier(jnp.mean(heads_view * heads_view, axis=-1, keepdims=True)) + 1e-06)
    normed = heads_view / rms
    inner = lax.optimization_barrier(jnp.mean(grads_view * normed, axis=-1, keepdims=True))
    return (normed.reshape(rows, -1), ((grads_view - normed * inner) / rms).reshape(rows, -1))

def one_replica(packed):
    tokens_x, upstream, weights, first, second = packed
    projected = jnp.dot(tokens_x, weights.astype(jnp.bfloat16), preferred_element_type=jnp.float32)
    normed, slopes = norm_backward(projected, upstream.astype(jnp.float32))
    slopes = slopes.astype(jnp.bfloat16)
    gradient = lax.dot_general(tokens_x, slopes, (((0,), (0,)), ((), ())), preferred_element_type=jnp.float32)
    moment_one = 0.9 * first + 0.1 * gradient
    moment_two = 0.95 * second + 0.05 * gradient * gradient
    stepped = weights - 0.4 * (moment_one / (jnp.sqrt(moment_two) + 1e-08) + 0.01 * weights)
    return (stepped, normed.astype(jnp.bfloat16))

def reference(inputs, cotangent, params, moment, second, drift, anchor, momentum):
    stepped, keys = lax.map(one_replica, (inputs, cotangent, params, moment, second))
    delta = lax.optimization_barrier(jnp.mean(drift.astype(jnp.float32), axis=0))
    momentum_new = 0.9 * momentum + delta
    anchor_new = anchor - 0.7 * (delta + 0.9 * momentum_new)
    merged = 0.3 * anchor_new[None] + 0.7 * stepped
    return (merged, keys, anchor_new, momentum_new)
```

```python
import jax
import jax.numpy as jnp
from jax import lax
from jax.experimental import pallas as pl
from jax.experimental.pallas import tpu as pltpu
from jax.sharding import PartitionSpec as P

HEAD_DIM = 128
ZS = 2
VMEM_LIMIT = 40 * 1024 * 1024
F32 = jnp.float32
BF16 = jnp.bfloat16


def spec(space):
    return pl.BlockSpec(memory_space=space)


def forward_body(ids, x_ref, cot_ref, *refs):
    chunks, (keys_ref, slopes_ref, w_ref) = refs[:-3], refs[-3:]
    rows = chunks[0].shape[0]
    for n, chunk in enumerate(chunks):
        at = pl.multiple_of(ids[n] * rows, 16)
        w_ref[pl.ds(at, rows), :] = chunk[...]
    wide = 2 * HEAD_DIM
    for col in range(0, w_ref.shape[1], wide):
        projected = jnp.dot(x_ref[...], w_ref[:, col : col + wide], preferred_element_type=F32)
        for head in range(0, wide, HEAD_DIM):
            p = projected[:, head : head + HEAD_DIM]
            inv = 1.0 / jnp.sqrt(jnp.mean(p * p, axis=-1, keepdims=True) + 1e-06)
            normed = p * inv
            g = cot_ref[:, col + head : col + head + HEAD_DIM].astype(F32)
            inner = jnp.mean(g * normed, axis=-1, keepdims=True)
            keys_ref[:, col + head : col + head + HEAD_DIM] = normed.astype(BF16)
            slopes_ref[:, col + head : col + head + HEAD_DIM] = ((g - normed * inner) * inv).astype(BF16)


def forward(ids, x, cot, chunks):
    out = jax.ShapeDtypeStruct(cot.shape, BF16)
    return pl.pallas_call(
        forward_body,
        out_shape=(out, out),
        in_specs=[spec(pltpu.SMEM)] + [spec(pltpu.VMEM)] * (2 + len(chunks)),
        out_specs=(spec(pltpu.VMEM), spec(pltpu.VMEM)),
        scratch_shapes=[pltpu.VMEM((x.shape[1], cot.shape[1]), BF16)],
        compiler_params=pltpu.CompilerParams(vmem_limit_bytes=VMEM_LIMIT),
        cost_estimate=pl.CostEstimate(flops=2 * x.shape[0] * x.shape[1] * cot.shape[1], bytes_accessed=7 << 20, transcendentals=0),
        name="forward",
    )(ids, x, cot, *chunks)


def partial_body(ids, xt_ref, slopes_ref, *outs):
    rows = outs[0].shape[0]
    for n, out in enumerate(outs):
        at = pl.multiple_of(ids[n] * rows, 16)
        out[...] = jnp.dot(xt_ref[pl.ds(at, rows), :], slopes_ref[...], preferred_element_type=F32).astype(BF16)


def partials(ids, xt, slopes, count, rows):
    out = jax.ShapeDtypeStruct((rows, slopes.shape[1]), BF16)
    return pl.pallas_call(
        partial_body,
        out_shape=(out,) * count,
        in_specs=[spec(pltpu.SMEM), spec(pltpu.VMEM), spec(pltpu.VMEM)],
        out_specs=(spec(pltpu.VMEM),) * count,
        compiler_params=pltpu.CompilerParams(vmem_limit_bytes=VMEM_LIMIT),
        cost_estimate=pl.CostEstimate(
            flops=2 * count * rows * slopes.size, bytes_accessed=(2 << 20) + count * rows * 2048, transcendentals=0
        ),
        name="partials",
    )(ids, xt, slopes)


def shards(inputs, cotangent, params, moment, second, drift, anchor, momentum):
    x, weights = inputs[0], params[0]
    rows = weights.shape[0]
    size = lax.axis_size("fsdp")
    ys = size // ZS
    index = lax.axis_index("fsdp").astype(jnp.int32)
    y, z = index // ZS, index % ZS
    half = ys // 2

    def step(value, dy, dz=0):
        pairs = [(a * ZS + b, ((a + dy) % ys) * ZS + (b + dz) % ZS) for a in range(ys) for b in range(ZS)]
        return lax.ppermute(value, "fsdp", pairs)

    def owner(dy, dz):
        return ((y + dy) % ys) * ZS + (z + dz) % ZS

    reps = lax.axis_size("rep")
    width = anchor.shape[1]
    sent = drift[0].T.reshape(reps, width, rows)
    drifts = lax.all_to_all(sent, "rep", split_axis=0, concat_axis=0, tiled=True)
    delta = jnp.sum(drifts.astype(F32), axis=0) / reps
    momentum_new = 0.9 * momentum.T + delta
    anchor_new = anchor.T - 0.7 * (delta + 0.9 * momentum_new)
    copies = jnp.broadcast_to(anchor_new.astype(BF16)[None], (reps, width, rows))
    anchors = lax.all_to_all(copies, "rep", split_axis=0, concat_axis=0, tiled=True)
    anchor_wide = anchors.reshape(reps * width, rows).T.astype(F32)

    own = weights.astype(BF16)
    other = step(own, 0, 1)
    chunks, where = [own, other], [owner(0, 0), owner(0, 1)]
    for dz, first, last in ((0, own, 1), (1, other, -1)):
        for way in (1, -1):
            held = first
            for hop in range(1, half + (way == last)):
                held = step(held, way)
                chunks.append(held)
                where.append(owner(-way * hop, dz))
    keys, slopes = forward(jnp.stack(where), x, cotangent[0], chunks)

    xt = x.T
    far = partials(jnp.stack([owner(half, 1), owner(half, 0)]), xt, slopes, 2, rows)
    order = [(0, 0), (0, 1)] + [(s * hop, dz) for hop in range(1, half) for s in (1, -1) for dz in (1, 0)]
    parts = partials(jnp.stack([owner(*o) for o in order]), xt, slopes, len(order), rows)
    part = dict(zip(order, parts))
    sums = {}
    for dz, first, last in ((1, far[0], -1), (0, far[1], 1)):
        total = part[0, dz].astype(F32)
        for way in (1, -1):
            held = step(first, way) if way == last else None
            for hop in range(half - 1, 0, -1):
                mine = part[way * hop, dz]
                if held is not None:
                    mine = (mine.astype(F32) + held.astype(F32)).astype(BF16)
                held = step(mine, way)
            total = total + held.astype(F32)
        sums[dz] = total
    gradient = sums[0] + step(sums[1].astype(BF16), 0, 1).astype(F32)

    moment_one = 0.9 * moment[0] + 0.1 * gradient
    moment_two = 0.95 * second[0] + 0.05 * gradient * gradient
    stepped = weights - 0.4 * (moment_one / (jnp.sqrt(moment_two) + 1e-08) + 0.01 * weights)
    merged = 0.3 * anchor_wide + 0.7 * stepped
    return (merged[None], keys[None], anchor_new.T, momentum_new.T)


def solution(mesh):
    return jax.shard_map(
        shards,
        mesh=mesh,
        in_specs=(
            P("rep", "fsdp", None),
            P("rep", "fsdp", None),
            P("rep", "fsdp", None),
            P("rep", "fsdp", None),
            P("rep", "fsdp", None),
            P("rep", "fsdp", None),
            P("fsdp", "rep"),
            P("fsdp", "rep"),
        ),
        out_specs=(
            P("rep", "fsdp", None),
            P("rep", "fsdp", None),
            P("fsdp", "rep"),
            P("fsdp", "rep"),
        ),
        check_vma=False,
    )
```

```python
import functools

import jax
import jax.numpy as jnp
from jax import lax
from jax.experimental import pallas as pl
from jax.experimental.pallas import tpu as pltpu
from jax.sharding import PartitionSpec as P

HEAD_DIM = 128
ZS = 2
VMEM_LIMIT = 16 * 1024 * 1024
F32 = jnp.float32
BF16 = jnp.bfloat16


def after(value, *others):
    return lax.optimization_barrier((value, *others))[0]


def spec(space):
    return pl.BlockSpec(memory_space=space)


TURNED = (((0,), (0,)), ((), ()))


def product_body(first, ids, mine_ref, theirs_ref, *refs):
    chunks, (own_ref, partner_ref, w_ref) = refs[:-3], refs[-3:]
    rows, cols = chunks[0].shape[0], own_ref.shape[1]
    for n, chunk in enumerate(chunks):
        at = pl.multiple_of(ids[n] * rows, 16)
        w_ref[pl.ds(at, rows), :] = chunk[:, first : first + cols]
    partner_ref[...] = lax.dot_general(theirs_ref[...], w_ref[...], TURNED, preferred_element_type=F32).astype(BF16)
    own_ref[...] = lax.dot_general(mine_ref[...], w_ref[...], TURNED, preferred_element_type=F32)


def product(first, cols, ids, mine, theirs, chunks):
    tokens = mine.shape[1]
    return pl.pallas_call(
        functools.partial(product_body, first),
        out_shape=(jax.ShapeDtypeStruct((tokens, cols), F32), jax.ShapeDtypeStruct((tokens, cols), BF16)),
        in_specs=[spec(pltpu.SMEM)] + [spec(pltpu.VMEM)] * (2 + len(chunks)),
        out_specs=(spec(pltpu.VMEM),) * 2,
        scratch_shapes=[pltpu.VMEM((mine.shape[0], cols), BF16)],
        compiler_params=pltpu.CompilerParams(vmem_limit_bytes=VMEM_LIMIT),
        cost_estimate=pl.CostEstimate(flops=4 * mine.size * cols, bytes_accessed=4 << 20, transcendentals=0),
        name="product",
    )(ids, mine, theirs, *chunks)


def norm_body(first, own_ref, other_ref, cot_ref, keys_ref, slopes_ref):
    for head in range(0, own_ref.shape[1], HEAD_DIM):
        at = slice(head, head + HEAD_DIM)
        p = own_ref[:, at] + other_ref[:, at].astype(F32)
        inv = 1.0 / jnp.sqrt(jnp.mean(p * p, axis=-1, keepdims=True) + 1e-06)
        normed = p * inv
        g = cot_ref[:, first + head : first + head + HEAD_DIM].astype(F32)
        inner = jnp.mean(g * normed, axis=-1, keepdims=True)
        keys_ref[:, at] = normed.astype(BF16)
        slopes_ref[:, at] = ((g - normed * inner) * inv).astype(BF16)


def norm(first, own, other, cot):
    out = jax.ShapeDtypeStruct(own.shape, BF16)
    return pl.pallas_call(
        functools.partial(norm_body, first),
        out_shape=(out, out),
        in_specs=[spec(pltpu.VMEM)] * 3,
        out_specs=(spec(pltpu.VMEM),) * 2,
        compiler_params=pltpu.CompilerParams(vmem_limit_bytes=VMEM_LIMIT),
        cost_estimate=pl.CostEstimate(flops=own.size * 16, bytes_accessed=own.size * 12, transcendentals=0),
        name="norm",
    )(own, other, cot)


def partial_body(pieces, rows, ids, mine_ref, theirs_ref, *refs):
    slopes, outs = refs[: 2 * pieces], refs[2 * pieces :]
    cols = slopes[0].shape[1]
    for n, out in enumerate(outs):
        at = pl.multiple_of(ids[n] * rows, 16)
        for k in range(pieces):
            total = jnp.dot(mine_ref[pl.ds(at, rows), :], slopes[k][...], preferred_element_type=F32)
            total += jnp.dot(theirs_ref[pl.ds(at, rows), :], slopes[pieces + k][...], preferred_element_type=F32)
            out[:, k * cols : (k + 1) * cols] = total.astype(BF16)


def partials(rows, ids, mine, theirs, slopes, swapped):
    width = sum(s.shape[1] for s in slopes)
    out = jax.ShapeDtypeStruct((rows, width), BF16)
    return pl.pallas_call(
        functools.partial(partial_body, len(slopes), rows),
        out_shape=(out,) * len(ids),
        in_specs=[spec(pltpu.SMEM)] + [spec(pltpu.VMEM)] * (2 + 2 * len(slopes)),
        out_specs=(spec(pltpu.VMEM),) * len(ids),
        compiler_params=pltpu.CompilerParams(vmem_limit_bytes=VMEM_LIMIT),
        cost_estimate=pl.CostEstimate(
            flops=4 * len(ids) * rows * 256 * width, bytes_accessed=(2 << 20) + len(ids) * rows * 2048, transcendentals=0
        ),
        name="partials",
    )(jnp.stack(ids), mine, theirs, *slopes, *swapped)


def add_body(rows, plan, *refs):
    out_ref = refs[-1]
    for n, terms in enumerate(plan):
        blocks = [refs[i][row : row + rows, :] for i, row in terms]
        total = blocks[0]
        if len(blocks) > 1:
            total = sum(b.astype(F32) for b in blocks[1:]) + total.astype(F32)
        out_ref[n * rows : (n + 1) * rows, :] = total.astype(BF16)


def add(rows, plan, *inputs):
    height = rows * len(plan)
    return pl.pallas_call(
        functools.partial(add_body, rows, plan),
        out_shape=jax.ShapeDtypeStruct((height, inputs[0].shape[1]), BF16),
        in_specs=[spec(pltpu.VMEM)] * len(inputs),
        out_specs=spec(pltpu.VMEM),
        compiler_params=pltpu.CompilerParams(vmem_limit_bytes=8 * 1024 * 1024),
        cost_estimate=pl.CostEstimate(flops=height * 1024, bytes_accessed=height * 4096, transcendentals=0),
        name="add",
    )(*inputs)


def shards(inputs, cotangent, params, moment, second, drift, anchor, momentum):
    x, weights = inputs[0], params[0]
    rows = weights.shape[0]
    size = lax.axis_size("fsdp")
    ys = size // ZS
    index = lax.axis_index("fsdp").astype(jnp.int32)
    y, z = index // ZS, index % ZS
    half = ys // 2

    def step(value, dy, dz=0):
        pairs = [(i * ZS + j, ((i + dy) % ys) * ZS + (j + dz) % ZS) for i in range(ys) for j in range(ZS)]
        return lax.ppermute(value, "fsdp", pairs)

    def at(k):
        return (y + k) % ys

    own = weights.astype(BF16)
    blocks = x.T.reshape(ys, ZS, rows, x.shape[0])
    mine = lax.dynamic_index_in_dim(blocks, z, 1, False).reshape(ys * rows, x.shape[0])
    theirs = lax.dynamic_index_in_dim(blocks, 1 - z, 1, False).reshape(ys * rows, x.shape[0])
    leaving = theirs
    theirs = step(leaving, 0, 1)

    reps = lax.axis_size("rep")
    width = anchor.shape[1]
    sent = after(drift[0], leaving).T.reshape(reps, width, rows)
    drifts = lax.all_to_all(sent, "rep", split_axis=0, concat_axis=0, tiled=True)
    delta = jnp.sum(drifts.astype(F32), axis=0) / reps
    momentum_new = 0.9 * momentum.T + delta
    anchor_new = anchor.T - 0.7 * (delta + 0.9 * momentum_new)
    copies = jnp.broadcast_to(anchor_new.astype(BF16)[None], (reps, width, rows))

    ups, downs = [step(own, 1)], [step(own, -1)]
    for n in range(half - 2):
        ups.append(step(after(ups[-1], leaving) if n == 0 else ups[-1], 1))
        downs.append(step(after(downs[-1], leaving) if n == 0 else downs[-1], -1))
    ups.append(step(after(ups[-1], theirs), 1))
    chunks = [own] + ups + downs
    where = jnp.stack([at(0)] + [at(-1 - n) for n in range(half)] + [at(1 + n) for n in range(half - 1)])
    where, copies = lax.optimization_barrier((where, copies))

    cols = weights.shape[1] // 2
    own1, out1 = product(0, cols, where, mine, theirs, chunks)
    in1 = step(out1, 0, 1)
    own2, out2 = product(cols, cols, where, mine, theirs, chunks)
    in2 = step(out2, 0, 1)
    keys1, slopes1 = norm(0, own1, in1, cotangent[0])
    swapped1 = step(slopes1, 0, 1)
    keys2, slopes2 = norm(cols, own2, in2, cotangent[0])
    swapped2 = step(slopes2, 0, 1)
    keys = jnp.concatenate([keys1, keys2], axis=1)
    copies = after(copies, in1)
    anchors = lax.all_to_all(copies, "rep", split_axis=0, concat_axis=0, tiled=True)

    slopes, swapped = (slopes1, slopes2), (swapped1, swapped2)
    order = [half, 1 - half] + [s * k for k in range(half - 1, 0, -1) for s in (1, -1) if s * k != 1 - half] + [0]
    part = dict(zip(order[:2], partials(rows, [at(k) for k in order[:2]], mine, theirs, slopes, swapped)))
    part.update(zip(order[2:], partials(rows, [at(k) for k in order[2:]], mine, theirs, slopes, swapped)))
    two = [[(0, 0), (1, 0)]]
    au, ad = step(part[half], 1), step(part[1 - half], -1)
    rest = lax.optimization_barrier(0.3 * anchors.reshape(reps * width, rows).T.astype(F32))
    for k in range(half - 1, 0, -1):
        if k == half - 2:
            part[k] = after(part[k], rest)
        au = step(add(rows, two, part[k], au), 1)
        if k > 1:
            ad = step(add(rows, two, part[1 - k], ad), -1)
    gradient = part[0].astype(F32) + au.astype(F32) + ad.astype(F32)

    moment_one = 0.9 * moment[0] + 0.1 * gradient
    moment_two = 0.95 * second[0] + 0.05 * gradient * gradient
    stepped = weights - 0.4 * (moment_one / (jnp.sqrt(moment_two) + 1e-08) + 0.01 * weights)
    merged = rest + 0.7 * stepped
    return (merged[None], keys[None], anchor_new.T, momentum_new.T)


def solution(mesh):
    return jax.shard_map(
        shards,
        mesh=mesh,
        in_specs=(
            P("rep", "fsdp", None),
            P("rep", "fsdp", None),
            P("rep", "fsdp", None),
            P("rep", "fsdp", None),
            P("rep", "fsdp", None),
            P("rep", "fsdp", None),
            P("fsdp", "rep"),
            P("fsdp", "rep"),
        ),
        out_specs=(
            P("rep", "fsdp", None),
            P("rep", "fsdp", None),
            P("fsdp", "rep"),
            P("fsdp", "rep"),
        ),
        check_vma=False,
    )
```

```python
import functools

import jax
import jax.numpy as jnp
from jax import lax
from jax.experimental import pallas as pl
from jax.experimental.pallas import tpu as pltpu
from jax.sharding import PartitionSpec as P

HEAD_DIM = 128
ZS = 2
VMEM_LIMIT = 16 * 1024 * 1024
F32 = jnp.float32
BF16 = jnp.bfloat16


def after(value, *others):
    return lax.optimization_barrier((value, *others))[0]


def spec(space):
    return pl.BlockSpec(memory_space=space)


TURNED = (((0,), (0,)), ((), ()))


def product_body(first, ids, mine_ref, theirs_ref, *refs):
    chunks, (own_ref, partner_ref, w_ref) = refs[:-3], refs[-3:]
    rows, cols = chunks[0].shape[0], own_ref.shape[1]
    for n, chunk in enumerate(chunks):
        at = pl.multiple_of(ids[n] * rows, 16)
        w_ref[pl.ds(at, rows), :] = chunk[:, first : first + cols]
    partner_ref[...] = lax.dot_general(theirs_ref[...], w_ref[...], TURNED, preferred_element_type=F32).astype(BF16)
    own_ref[...] = lax.dot_general(mine_ref[...], w_ref[...], TURNED, preferred_element_type=F32)


def product(first, cols, ids, mine, theirs, chunks):
    tokens = mine.shape[1]
    return pl.pallas_call(
        functools.partial(product_body, first),
        out_shape=(jax.ShapeDtypeStruct((tokens, cols), F32), jax.ShapeDtypeStruct((tokens, cols), BF16)),
        in_specs=[spec(pltpu.SMEM)] + [spec(pltpu.VMEM)] * (2 + len(chunks)),
        out_specs=(spec(pltpu.VMEM),) * 2,
        scratch_shapes=[pltpu.VMEM((mine.shape[0], cols), BF16)],
        compiler_params=pltpu.CompilerParams(vmem_limit_bytes=VMEM_LIMIT),
        cost_estimate=pl.CostEstimate(flops=4 * mine.size * cols, bytes_accessed=4 << 20, transcendentals=0),
        name="product",
    )(ids, mine, theirs, *chunks)


def norm_body(first, own_ref, other_ref, cot_ref, keys_ref, slopes_ref):
    for head in range(0, own_ref.shape[1], HEAD_DIM):
        at = slice(head, head + HEAD_DIM)
        p = own_ref[:, at] + other_ref[:, at].astype(F32)
        inv = 1.0 / jnp.sqrt(jnp.mean(p * p, axis=-1, keepdims=True) + 1e-06)
        normed = p * inv
        g = cot_ref[:, first + head : first + head + HEAD_DIM].astype(F32)
        inner = jnp.mean(g * normed, axis=-1, keepdims=True)
        keys_ref[:, at] = normed.astype(BF16)
        slopes_ref[:, at] = ((g - normed * inner) * inv).astype(BF16)


def norm(first, own, other, cot):
    out = jax.ShapeDtypeStruct(own.shape, BF16)
    return pl.pallas_call(
        functools.partial(norm_body, first),
        out_shape=(out, out),
        in_specs=[spec(pltpu.VMEM)] * 3,
        out_specs=(spec(pltpu.VMEM),) * 2,
        compiler_params=pltpu.CompilerParams(vmem_limit_bytes=VMEM_LIMIT),
        cost_estimate=pl.CostEstimate(flops=own.size * 16, bytes_accessed=own.size * 12, transcendentals=0),
        name="norm",
    )(own, other, cot)


def partial_body(pieces, rows, ids, mine_ref, theirs_ref, *refs):
    slopes, outs = refs[: 2 * pieces], refs[2 * pieces :]
    cols = slopes[0].shape[1]
    for n, out in enumerate(outs):
        at = pl.multiple_of(ids[n] * rows, 16)
        for k in range(pieces):
            total = jnp.dot(mine_ref[pl.ds(at, rows), :], slopes[k][...], preferred_element_type=F32)
            total += jnp.dot(theirs_ref[pl.ds(at, rows), :], slopes[pieces + k][...], preferred_element_type=F32)
            out[:, k * cols : (k + 1) * cols] = total.astype(BF16)


def partials(rows, ids, mine, theirs, slopes, swapped):
    width = sum(s.shape[1] for s in slopes)
    out = jax.ShapeDtypeStruct((rows, width), BF16)
    return pl.pallas_call(
        functools.partial(partial_body, len(slopes), rows),
        out_shape=(out,) * len(ids),
        in_specs=[spec(pltpu.SMEM)] + [spec(pltpu.VMEM)] * (2 + 2 * len(slopes)),
        out_specs=(spec(pltpu.VMEM),) * len(ids),
        compiler_params=pltpu.CompilerParams(vmem_limit_bytes=VMEM_LIMIT),
        cost_estimate=pl.CostEstimate(
            flops=4 * len(ids) * rows * 256 * width, bytes_accessed=(2 << 20) + len(ids) * rows * 2048, transcendentals=0
        ),
        name="partials",
    )(jnp.stack(ids), mine, theirs, *slopes, *swapped)


def add_body(rows, plan, *refs):
    out_ref = refs[-1]
    for n, terms in enumerate(plan):
        blocks = [refs[i][row : row + rows, :] for i, row in terms]
        total = blocks[0]
        if len(blocks) > 1:
            total = sum(b.astype(F32) for b in blocks[1:]) + total.astype(F32)
        out_ref[n * rows : (n + 1) * rows, :] = total.astype(BF16)


def add(rows, plan, *inputs):
    height = rows * len(plan)
    return pl.pallas_call(
        functools.partial(add_body, rows, plan),
        out_shape=jax.ShapeDtypeStruct((height, inputs[0].shape[1]), BF16),
        in_specs=[spec(pltpu.VMEM)] * len(inputs),
        out_specs=spec(pltpu.VMEM),
        compiler_params=pltpu.CompilerParams(vmem_limit_bytes=8 * 1024 * 1024),
        cost_estimate=pl.CostEstimate(flops=height * 1024, bytes_accessed=height * 4096, transcendentals=0),
        name="add",
    )(*inputs)


def shards(inputs, cotangent, params, moment, second, drift, anchor, momentum):
    x, weights = inputs[0], params[0]
    rows = weights.shape[0]
    size = lax.axis_size("fsdp")
    ys = size // ZS
    index = lax.axis_index("fsdp").astype(jnp.int32)
    y, z = index // ZS, index % ZS
    half = ys // 2

    def step(value, dy, dz=0):
        pairs = [(i * ZS + j, ((i + dy) % ys) * ZS + (j + dz) % ZS) for i in range(ys) for j in range(ZS)]
        return lax.ppermute(value, "fsdp", pairs)

    def at(k):
        return (y + k) % ys

    own = weights.astype(BF16)
    blocks = x.T.reshape(ys, ZS, rows, x.shape[0])
    theirs = lax.dynamic_index_in_dim(blocks, 1 - z, 1, False).reshape(ys * rows, x.shape[0])
    leaving = theirs
    theirs = step(leaving, 0, 1)
    mine = lax.dynamic_index_in_dim(after(blocks, theirs), z, 1, False).reshape(ys * rows, x.shape[0])

    reps = lax.axis_size("rep")
    width = anchor.shape[1]
    sent = after(drift[0], leaving).T.reshape(reps, width, rows)
    drifts = lax.all_to_all(sent, "rep", split_axis=0, concat_axis=0, tiled=True)

    ups, downs = [step(own, 1)], [step(own, -1)]
    for n in range(half - 2):
        ups.append(step(after(ups[-1], leaving) if n == 0 else ups[-1], 1))
        downs.append(step(after(downs[-1], leaving) if n == 0 else downs[-1], -1))
    ups.append(step(after(ups[-1], theirs), 1))
    chunks = [own] + ups + downs
    where = jnp.stack([at(0)] + [at(-1 - n) for n in range(half)] + [at(1 + n) for n in range(half - 1)])

    cols = weights.shape[1] // 2
    own1, out1 = product(0, cols, where, mine, theirs, chunks)
    in1 = step(out1, 0, 1)
    drifts = after(drifts, out1)
    delta = jnp.sum(drifts.astype(F32), axis=0) / reps
    momentum_new = 0.9 * momentum.T + delta
    anchor_new = anchor.T - 0.7 * (delta + 0.9 * momentum_new)
    copies = jnp.broadcast_to(anchor_new.astype(BF16)[None], (reps, width, rows))
    own2, out2 = product(cols, cols, where, mine, theirs, chunks)
    in2 = step(out2, 0, 1)
    keys1, slopes1 = norm(0, own1, in1, cotangent[0])
    swapped1 = step(slopes1, 0, 1)
    keys2, slopes2 = norm(cols, own2, in2, cotangent[0])
    swapped2 = step(slopes2, 0, 1)
    keys = jnp.concatenate([keys1, keys2], axis=1)
    copies = after(copies, in1)
    anchors = lax.all_to_all(copies, "rep", split_axis=0, concat_axis=0, tiled=True)

    slopes, swapped = (slopes1, slopes2), (swapped1, swapped2)
    order = [half, 1 - half] + [s * k for k in range(half - 1, 0, -1) for s in (1, -1) if s * k != 1 - half] + [0]
    part = dict(zip(order[:2], partials(rows, [at(k) for k in order[:2]], mine, theirs, slopes, swapped)))
    part.update(zip(order[2:], partials(rows, [at(k) for k in order[2:]], mine, theirs, slopes, swapped)))
    two = [[(0, 0), (1, 0)]]
    au, ad = step(part[half], 1), step(part[1 - half], -1)
    rest = lax.optimization_barrier(0.3 * anchors.reshape(reps * width, rows).T.astype(F32))
    for k in range(half - 1, 0, -1):
        if k == half - 2:
            part[k] = after(part[k], rest)
        au = step(add(rows, two, part[k], au), 1)
        if k > 1:
            ad = step(add(rows, two, part[1 - k], ad), -1)
    gradient = part[0].astype(F32) + au.astype(F32) + ad.astype(F32)

    moment_one = 0.9 * moment[0] + 0.1 * gradient
    moment_two = 0.95 * second[0] + 0.05 * gradient * gradient
    stepped = weights - 0.4 * (moment_one / (jnp.sqrt(moment_two) + 1e-08) + 0.01 * weights)
    merged = rest + 0.7 * stepped
    return (merged[None], keys[None], anchor_new.T, momentum_new.T)


def solution(mesh):
    return jax.shard_map(
        shards,
        mesh=mesh,
        in_specs=(
            P("rep", "fsdp", None),
            P("rep", "fsdp", None),
            P("rep", "fsdp", None),
            P("rep", "fsdp", None),
            P("rep", "fsdp", None),
            P("rep", "fsdp", None),
            P("fsdp", "rep"),
            P("fsdp", "rep"),
        ),
        out_specs=(
            P("rep", "fsdp", None),
            P("rep", "fsdp", None),
            P("fsdp", "rep"),
            P("fsdp", "rep"),
        ),
        check_vma=False,
    )
```
